256 devices in a mesh: ep: 64 (over x_hi, y, z), et: 4 (over x_lo, core).
Axes of the slice: x: 4 (x_hi: 2, x_lo: 2; x = x_hi * 2 + x_lo), y: 4, z: 8, core: 2. Of those that a mesh axis runs over, the one named last changes fastest.
Arguments:
- tokens: bfloat16 [8192, 3584], P('ep', 'et'), may hold values from -6 to 6
- slot_ids: int32 [8192, 8], P('ep'), may hold values from 0 to 63, all different within a row; in each aligned block of 128 rows (0 to 127, 128 to 255, ...) at most 20 rows name the same one
- gate_weights: float32 [8192, 8], P('ep'), may hold values from 0.1 to 1
- old_expert: int32 [64], replicated, may hold values from 0 to 55, as said below
- new_expert: int32 [64], replicated, may hold values from 0 to 55, as said below
- gate_proj: bfloat16 [64, 3584, 1024], P(None, 'ep', 'et'), may hold values from -0.09375 to 0.09375
- up_proj: bfloat16 [64, 3584, 1024], P(None, 'ep', 'et'), may hold values from -0.09375 to 0.09375
- down_proj: bfloat16 [64, 3584, 1024], P(None, 'ep', 'et'), may hold values from -0.1875 to 0.1875
Outputs:
- layer_out: bfloat16 [8192, 3584], P('ep', 'et')
The draws below stay inside these ranges and needn't reach their ends.
Inputs may be any that keep to these rules, and one draw needn't show every extreme that they name: `slot_ids`: each row names 8 different slots. The rows of one index of ep name no slot more than 20 times, and in every draw some slot exactly 20 times on some index. `old_expert`: names every expert 0 to 55 once or twice; 8 of them twice. `new_expert`: names every expert 0 to 55 once or twice; 8 of them twice.
All inputs are finite; a program needn't handle non-finite values.
Results may differ from the reference program's by a relative error of at most 0.015.
Values may be sent and summed in bfloat16 or wider, within the bound.
A program may use at most 128 MiB of HBM per device.

```python
import math
import jax
import jax.numpy as jnp
import numpy as np
from jax import lax

D = 3584
FF = 1024
TOP = 8
TOK_DEV = 128
SLOTS = 64
EXPERTS = 56
CAP = 20
TOKENS = 8192
N_EP = 64
N_ET = 4


def draw_old_expert(key, part):
    key = jax.random.fold_in(key, 11)
    ordering = jax.random.permutation(key, SLOTS)
    return (ordering % EXPERTS).astype(jnp.int32)


def draw_new_expert(key, part):
    key = jax.random.fold_in(key, 23)
    key_order, key_shift = jax.random.split(key)
    ordering = jax.random.permutation(key_order, SLOTS)
    offset = jax.random.randint(key_shift, (), 0, EXPERTS)
    return ((ordering % EXPERTS + offset) % EXPERTS).astype(jnp.int32)


def shard_levels(stream_key, shape, cuts, least, largest):
    gain = 1.0
    for dim, blocks in cuts:
        draws = jax.random.uniform(jax.random.fold_in(jax.random.fold_in(stream_key, 6), dim), (blocks,), jnp.float32, least / len(cuts), largest / len(cuts))
        gain = gain * jnp.repeat(jnp.exp(draws), shape[dim] // blocks).reshape((-1,) + (1,) * (len(shape) - 1 - dim))
    return gain


def assign_block(own_key, own, number, rows, amount, top, bound, slope):
    order = jax.random.permutation(own_key, amount)
    crowded, usual = load_shares(amount, rows * top, bound, slope, True), load_shares(amount, rows * top, bound, slope, False)
    places = jnp.arange(amount)

    def named(tallies, rotation):
        used = int((tallies > 0).sum())
        fixed = max(1, used // 4)
        moved = fixed + (places - fixed + rotation * (used - fixed)) % max(1, amount - fixed)
        return jnp.zeros((amount,), jnp.int32).at[order[jnp.where(places < fixed, places, moved)]].set(jnp.asarray(tallies, jnp.int32))

    tallies = jnp.where(number % 4 == 0, named(crowded, number // 4), named(usual, number - number // 4 - 1))
    mixed = jax.random.permutation(jax.random.fold_in(own, 3), amount)
    source_of, sink = mixed[0:amount // 2 * 2:2], mixed[1:amount // 2 * 2:2]
    margin = jnp.minimum(tallies[source_of] - 1, bound - tallies[sink]) // 2
    margin = jnp.where((source_of == order[0]) | (sink == order[0]) | (tallies[sink] == 0), 0, jnp.maximum(margin, 0))
    moved = jax.random.randint(jax.random.fold_in(own, 4), (amount // 2,), 0, 1 << 20) % (margin + 1)
    tallies = tallies.at[source_of].add(-moved).at[sink].add(moved)
    labels = jnp.searchsorted(jnp.cumsum(tallies), jnp.arange(rows * top), side="right").astype(jnp.int32)
    listing = labels.reshape(top, rows).T
    listing = listing[jax.random.permutation(jax.random.fold_in(own, 1), rows)]
    rotation = jax.random.randint(jax.random.fold_in(own, 2), (rows, 1), 0, top)
    return jnp.take_along_axis(listing, (jnp.arange(top)[None, :] + rotation) % top, axis=1)


def load_shares(number_of, total, most, skew, full):
    weights = [(1 << 20) // math.isqrt(standing ** skew) + 1 for standing in range(1, number_of + 1)]
    largest = most if full else min(most, max(-(-total // number_of), total * weights[0] // sum(weights)))
    least = 1 if total - largest >= number_of - 1 else 0
    counts, spare = [largest] + [least] * (number_of - 1), total - largest - least * (number_of - 1)
    while spare > 0:
        free = [i for i in range(1, number_of) if counts[i] < largest] or [i for i in range(1, number_of) if counts[i] < most]
        whole, remaining = sum([weights[i] for i in free]), spare
        for i in free:
            extra = min(most - counts[i], max(1, remaining * weights[i] // whole), spare)
            counts[i] = counts[i] + extra
            spare = spare - extra
    return np.array(counts)


def gaussian(key, extent, width, most, shards=(), kind=jnp.bfloat16):
    factor_of = shard_levels(key, extent, shards, -0.22, 0.18) if shards else 1.0
    array = jax.random.normal(key, extent, jnp.float32) * width * factor_of
    return jnp.minimum(jnp.maximum(array, -most), most).astype(kind)


def setup_inputs(seed: int = 0) -> dict:
    streams_of = jax.random.split(jax.random.key(seed), 9)
    tokens = gaussian(streams_of[0], (TOKENS, D), 1.0, 6.0, ((0, 64), (1, 4)))
    slot_ids_keys = jax.random.split(jax.random.fold_in(streams_of[1], 1), TOKENS // TOK_DEV)
    slot_ids_turns = jax.random.permutation(jax.random.fold_in(streams_of[1], 3), TOKENS // TOK_DEV)
    slot_ids = jax.vmap(lambda own, number: assign_block(jax.random.fold_in(streams_of[1], 2), own, number, TOK_DEV, SLOTS, TOP, CAP, 2))(slot_ids_keys, slot_ids_turns).reshape((TOKENS, TOP))
    gate_weights = jnp.clip(jnp.exp(math.log(1.0) - 2.3025851 * jax.random.uniform(streams_of[2], (TOKENS, TOP), jnp.float32) ** shard_levels(streams_of[2], (TOKENS, TOP), ((0, 64),), -0.2, 0.2)), 0.1, 1.0)
    old_expert = draw_old_expert(jax.random.fold_in(streams_of[8], 71), 0)
    new_expert = draw_new_expert(jax.random.fold_in(streams_of[8], 71), 0)
    gate_proj = gaussian(streams_of[5], (SLOTS, D, FF), D ** -0.5, 0.09375, ((1, 64), (2, 4)))
    up_proj = gaussian(streams_of[6], (SLOTS, D, FF), D ** -0.5, 0.09375, ((1, 64), (2, 4)))
    down_proj = gaussian(streams_of[7], (SLOTS, D, FF), FF ** -0.5, 0.1875, ((1, 64), (2, 4)))
    return dict(tokens=tokens, slot_ids=slot_ids, gate_weights=gate_weights, old_expert=old_expert, new_expert=new_expert, gate_proj=gate_proj, up_proj=up_proj, down_proj=down_proj)


def expert_rows(slot_rows, gate_slab, up_slab, down_slab):
    share_width = gate_slab.shape[1] // N_ET
    running = jnp.zeros((slot_rows.shape[0], down_slab.shape[0]), jnp.float32)
    for share in range(N_ET):
        offset = share * share_width
        gate_part = jnp.dot(slot_rows, gate_slab[:, offset:offset + share_width], preferred_element_type=jnp.float32)
        up_part = jnp.dot(slot_rows, up_slab[:, offset:offset + share_width], preferred_element_type=jnp.float32)
        hidden = (jax.nn.silu(gate_part) * up_part).astype(jnp.bfloat16)
        partial_value = jnp.dot(hidden, down_slab[:, offset:offset + share_width].T, preferred_element_type=jnp.float32)
        running = running + partial_value.astype(jnp.bfloat16).astype(jnp.float32)
    return running


def reference(tokens, slot_ids, gate_weights, old_expert, new_expert, gate_proj, up_proj, down_proj):
    slot_index = jnp.arange(SLOTS, dtype=jnp.int32)
    holders = new_expert[:, None] == old_expert[None, :]
    source = jnp.min(jnp.where(holders, slot_index[None, :], SLOTS), axis=1).astype(jnp.int32)
    flat_slot = slot_ids.reshape(-1)
    gate_pad = jnp.concatenate([gate_weights.reshape(-1), jnp.zeros((1,), jnp.float32)])
    padded = jnp.concatenate([tokens, jnp.zeros((1, D), tokens.dtype)], axis=0)
    row_limit = N_EP * CAP

    def one_slot(accumulated, slot_number):
        chosen = jnp.nonzero(flat_slot == slot_number, size=row_limit, fill_value=TOKENS * TOP)[0].astype(jnp.int32)
        token_row = (chosen // TOP).astype(jnp.int32)
        slot_rows = padded[token_row]
        anchor = source[slot_number]
        result = expert_rows(slot_rows, gate_proj[anchor], up_proj[anchor], down_proj[anchor])
        scaled = result * gate_pad[chosen][:, None]
        return accumulated.at[token_row].add(scaled), None

    start_sum = jnp.zeros((TOKENS + 1, D), jnp.float32)
    accumulated, unused = lax.scan(one_slot, start_sum, slot_index)
    return accumulated[:TOKENS].astype(jnp.bfloat16)
```

```python
import functools

import jax
import jax.numpy as jnp
from jax import lax
from jax.experimental import pallas as pl
from jax.experimental.pallas import tpu as pltpu
from jax.sharding import PartitionSpec as P

MESH = pl.DeviceIdType.MESH
NZ = 8
F32 = jnp.float32
BF16 = jnp.bfloat16


def layer_kernel(
    cap,
    source_ref, tokens_hbm, slot_t_ref, gate_t_ref, gate_hbm, up_hbm, down_hbm, out_ref,
    stage_gate, stage_up, stage_down, wsend, gu_recv, down_recv, idx_send, idx_recv, tok_all, pick, combine, row_send, rows_in,
    part_send, part_recv, own, hid, out_send, ret, zsend, zrecv,
    load_sem, wsend_sem, wrecv_sem, self_sem, tok_send_sem, tok_recv_sem, idx_send_sem, idx_recv_sem,
    row_send_sem, row_recv_sem, fwd_send_sem, fwd_recv_sem, part_send_sem, part_recv_sem,
    hid_send_sem, hid_recv_sem, out_send_sem, ret_recv_sem, z_send_sem, z_recv_sem,
):
    n_ep = stage_gate.shape[0]
    n_xy = n_ep // NZ
    tok = tok_all.shape[1]
    width = tok_all.shape[2]
    line_rows = NZ * cap
    n_rows = n_xy * line_rows
    ep = lax.axis_index("ep")
    et = lax.axis_index("et")
    me_xy, me_z = ep // NZ, ep % NZ
    h, c = et // 2, et % 2
    half = ep // (n_ep // 2)
    quarter = ep // (n_ep // 4)
    gu_et = half * 2 + c
    weights_hbm = (gate_hbm, up_hbm, down_hbm)
    stage = (stage_gate, stage_up, stage_down)

    loads = [
        pltpu.make_async_copy(weights_hbm[k], stage[k], load_sem.at[k]) for k in range(3)
    ]
    token_load = pltpu.make_async_copy(tokens_hbm, tok_all.at[me_z], load_sem.at[3])
    token_load.start()
    for load in loads:
        load.start()

    barrier = pltpu.get_barrier_semaphore()

    def greet(other_ep, other_et):
        pl.semaphore_signal(barrier, inc=1, device_id=(other_ep, other_et), device_id_type=MESH)

    @pl.loop(0, n_ep)
    def _(k):
        other_ep, other_et = h * (n_ep // 2) + k // 2, (k % 2) * 2 + c

        @pl.when(jnp.logical_or(other_ep != ep, other_et != et))
        def _():
            greet(other_ep, other_et)

    @pl.loop(0, n_ep)
    def _(k):
        other_ep, other_et = et * (n_ep // 4) + k // 4, k % 4

        @pl.when(jnp.logical_or(other_ep != ep, other_et != et))
        def _():
            greet(other_ep, other_et)

    for d in range(1, NZ):
        greet(me_xy * NZ + (me_z + d) % NZ, et)
    for d in range(1, n_xy):
        greet(((me_xy + d) % n_xy) * NZ + me_z, et)
    for d in range(1, 4):
        greet(ep, (et + d) % 4)

    row = lax.broadcasted_iota(jnp.int32, (n_ep, tok), 0)
    row_slot = (row % n_xy) * NZ + row // n_xy
    named = jnp.zeros((n_ep, tok), F32)
    weight = jnp.zeros((n_ep, tok), F32)
    for k in range(slot_t_ref.shape[0]):
        hit = slot_t_ref[k : k + 1, :] == row_slot
        named = jnp.where(hit, 1.0, named)
        weight = jnp.where(hit, gate_t_ref[k : k + 1, :], weight)
    earlier = (
        lax.broadcasted_iota(jnp.int32, (tok, tok), 0) < lax.broadcasted_iota(jnp.int32, (tok, tok), 1)
    )
    place = jnp.dot(
        named.astype(BF16), jnp.where(earlier, 1.0, 0.0).astype(BF16), preferred_element_type=F32
    )
    place = jnp.where(named > 0.5, place, -100000.0)
    for z in range(NZ):
        idx_send[z, 0:n_xy, :] = place[z * n_xy : (z + 1) * n_xy]
        idx_send[z, n_xy : 2 * n_xy, :] = weight[z * n_xy : (z + 1) * n_xy]
    idx_recv[me_z] = idx_send[me_z]
    token_load.wait()

    same = jnp.where(gu_et == et, 1, 0)
    same_down = jnp.where(quarter == et, 1, 0)
    pl.semaphore_wait(barrier, 2 * n_ep - same - same_down + (NZ - 1) + (n_xy - 1) + 3)

    def token_copy(d):
        peer = me_xy * NZ + (me_z + d) % NZ
        return pltpu.make_async_remote_copy(
            tok_all.at[me_z], tok_all.at[me_z], tok_send_sem.at[d], tok_recv_sem.at[d],
            device_id=(peer, et), device_id_type=MESH,
        )

    def index_copy(d):
        peer_z = (me_z + d) % NZ
        return pltpu.make_async_remote_copy(
            idx_send.at[peer_z], idx_recv.at[me_z], idx_send_sem.at[d], idx_recv_sem.at[d],
            device_id=(me_xy * NZ + peer_z, et), device_id_type=MESH,
        )

    for d in range(1, NZ):
        index_copy(d).start()
        token_copy(d).start()

    def weight_target(k):
        if k < 2:
            return gu_et, gu_recv.at[k, et // 2, ep % (n_ep // 2)]
        return quarter, down_recv.at[et, ep % (n_ep // 4)]

    def send_weights(k):
        target_et, target = weight_target(k)

        @pl.loop(0, n_ep)
        def _(d):
            slot = (ep + d) % n_ep
            wsend[k, slot] = stage[k][source_ref[slot]]

            @pl.when(jnp.logical_or(slot != ep, target_et != et))
            def _():
                pltpu.make_async_remote_copy(
                    wsend.at[k, slot], target, wsend_sem.at[k], wrecv_sem.at[k],
                    device_id=(slot, target_et), device_id_type=MESH,
                ).start()

            @pl.when(jnp.logical_and(slot == ep, target_et == et))
            def _():
                pltpu.make_async_copy(wsend.at[k, slot], target, wrecv_sem.at[k]).start()

    def wait_weights(k):
        landed = gu_recv.at[k] if k < 2 else down_recv
        pltpu.make_async_copy(landed, landed, wrecv_sem.at[k]).wait()

    def wait_weights_sent(k):
        target_et, target = weight_target(k)

        @pl.loop(0, n_ep)
        def _(slot):
            @pl.when(jnp.logical_or(slot != ep, target_et != et))
            def _():
                pltpu.make_async_remote_copy(
                    wsend.at[k, slot], target, wsend_sem.at[k], wrecv_sem.at[k],
                    device_id=(slot, target_et), device_id_type=MESH,
                ).wait_send()

    loads[0].wait()
    send_weights(0)

    for d in range(1, NZ):
        index_copy(d).wait_recv()
        token_copy(d).wait_recv()
    line_row = lax.broadcasted_iota(jnp.int32, (line_rows, tok), 0).astype(F32)

    def row_copy(d):
        peer_xy = (me_xy + d) % n_xy
        return pltpu.make_async_remote_copy(
            row_send.at[peer_xy], rows_in.at[c, me_xy], row_send_sem.at[d], row_recv_sem.at[d],
            device_id=(peer_xy * NZ + me_z, et), device_id_type=MESH,
        )

    for d in range(1, n_xy + 1):
        j = (me_xy + d) % n_xy
        for z in range(NZ):
            line = idx_recv[z, pl.ds(j, 1), :] + float(z * cap)
            pick[:, z * tok : (z + 1) * tok] = jnp.where(line == line_row, 1.0, 0.0).astype(BF16)
        rows = jnp.dot(
            pick[...], tok_all[...].reshape(NZ * tok, width), preferred_element_type=F32
        ).astype(BF16)
        if d < n_xy:
            row_send[j] = rows
            row_copy(d).start()
        else:
            rows_in[c, me_xy] = rows

    loads[1].wait()
    send_weights(1)

    def forward_copy(d):
        place_xy = (me_xy + n_xy - d) % n_xy
        return pltpu.make_async_remote_copy(
            rows_in.at[c, place_xy], rows_in.at[c, place_xy], fwd_send_sem.at[d], fwd_recv_sem.at[d],
            device_id=(ep, et + 1 - 2 * c), device_id_type=MESH,
        )

    def forward_landing(d):
        place_xy = (me_xy + n_xy - d) % n_xy
        return pltpu.make_async_remote_copy(
            rows_in.at[1 - c, place_xy], rows_in.at[1 - c, place_xy], fwd_send_sem.at[d],
            fwd_recv_sem.at[d], device_id=(ep, et + 1 - 2 * c), device_id_type=MESH,
        )

    for d in range(n_xy):
        if d > 0:
            row_copy(d).wait_recv()
        forward_copy(d).start()

    loads[2].wait()
    send_weights(2)

    lane = lax.broadcasted_iota(jnp.int32, (tok, n_rows), 1).astype(F32)

    @pl.loop(0, NZ)
    def _(z):
        columns = idx_recv[z].T
        total = jnp.zeros((tok, n_rows), F32)
        for j in range(n_xy):
            at = columns[:, j : j + 1] + (j * line_rows + z * cap).astype(F32)
            total = jnp.where(at == lane, columns[:, n_xy + j : n_xy + j + 1], total)
        combine[z] = total.astype(BF16)

    for d in range(n_xy):
        forward_landing(d).wait_recv()

    n_part = part_send_sem.shape[1]
    part_rows = n_rows // n_part
    chunk_lines = n_xy // n_part
    block = own.shape[2]

    def product(k, b, q):
        total = jnp.zeros((part_rows, block), F32)
        for cc in range(2):
            left = rows_in[cc, pl.ds(q * chunk_lines, chunk_lines)].reshape(part_rows, width)
            right = gu_recv[k, b, pl.ds(cc * (n_ep // 4), n_ep // 4)].reshape(width, block)
            total = total + jnp.dot(left, right, preferred_element_type=F32)
        return total

    def part_copy(k, q):
        where = pl.ds(q * part_rows, part_rows)
        return pltpu.make_async_remote_copy(
            part_send.at[k, where], part_recv.at[k, where], part_send_sem.at[k, q], part_recv_sem.at[k, q],
            device_id=(ep, (et + 2) % 4), device_id_type=MESH,
        )

    for k in range(2):
        wait_weights(k)

        @pl.loop(0, n_part)
        def _(q):
            where = pl.ds(pl.multiple_of(q * part_rows, part_rows), part_rows)
            part_send[k, where] = product(k, 1 - h, q).astype(BF16)
            part_copy(k, q).start()

        @pl.loop(0, n_part)
        def _(q):
            where = pl.ds(pl.multiple_of(q * part_rows, part_rows), part_rows)
            own[k, where] = product(k, h, q)

    def hidden_copy(d, q):
        where = pl.ds(q * part_rows, part_rows)
        return pltpu.make_async_remote_copy(
            hid.at[et, where], hid.at[et, where], hid_send_sem.at[d, q], hid_recv_sem.at[d, q],
            device_id=(ep, (et + d) % 4), device_id_type=MESH,
        )

    @pl.loop(0, n_part)
    def _(q):
        where = pl.ds(pl.multiple_of(q * part_rows, part_rows), part_rows)
        part_copy(0, q).wait_recv()
        part_copy(1, q).wait_recv()
        g = own[0, where] + part_recv[0, where].astype(F32)
        u = own[1, where] + part_recv[1, where].astype(F32)
        hid[et, where] = (g / (1.0 + jnp.exp(-g)) * u).astype(BF16)
        for d in range(1, 4):
            hidden_copy(d, q).start()

    wait_weights(2)

    def out_copy(i, d):
        return pltpu.make_async_remote_copy(
            out_send.at[i], ret.at[me_xy], out_send_sem.at[d], ret_recv_sem.at[d],
            device_id=(i * NZ + me_z, et), device_id_type=MESH,
        )

    def down_chunk(q):
        for d in range(1, 4):
            hidden_copy(d, q).wait_recv()
        where = pl.ds(pl.multiple_of(q * part_rows, part_rows), part_rows)
        total = jnp.zeros((part_rows, width), F32)
        for k in range(4):
            right = down_recv[k].reshape(width, block)
            total = total + lax.dot_general(
                hid[k, where], right, (((1,), (1,)), ((), ())), preferred_element_type=F32
            )
        total = total.astype(BF16)
        for v in range(chunk_lines):
            i = q * chunk_lines + v
            rows = total[v * line_rows : (v + 1) * line_rows]
            d = (i - me_xy + n_xy) % n_xy

            @pl.when(d == 0)
            def _():
                ret[me_xy] = rows

            @pl.when(d != 0)
            def _():
                out_send[i] = rows
                out_copy(i, d).start()

    @pl.loop(0, n_part)
    def _(q):
        down_chunk(q)

    for d in range(1, n_xy):
        out_copy((me_xy + d) % n_xy, d).wait_recv()

    def sum_copy(d):
        peer_z = (me_z + d) % NZ
        return pltpu.make_async_remote_copy(
            zsend.at[peer_z], zrecv.at[me_z], z_send_sem.at[d], z_recv_sem.at[d],
            device_id=(me_xy * NZ + peer_z, et), device_id_type=MESH,
        )

    @pl.loop(1, NZ + 1)
    def _(d):
        z = (me_z + d) % NZ
        total = jnp.dot(
            combine[z], ret[...].reshape(n_rows, width), preferred_element_type=F32
        ).astype(BF16)

        @pl.when(d < NZ)
        def _():
            zsend[z] = total
            sum_copy(d).start()

        @pl.when(d == NZ)
        def _():
            zrecv[me_z] = total

    for d in range(1, NZ):
        sum_copy(d).wait_recv()
    result = zrecv[0].astype(F32)
    for z in range(1, NZ):
        result = result + zrecv[z].astype(F32)
    out_ref[...] = result.astype(BF16)

    for d in range(1, NZ):
        index_copy(d).wait_send()
        token_copy(d).wait_send()
        sum_copy(d).wait_send()
    for d in range(1, n_xy):
        row_copy(d).wait_send()
        out_copy((me_xy + d) % n_xy, d).wait_send()
    for d in range(n_xy):
        forward_copy(d).wait_send()
    for k in range(3):
        wait_weights_sent(k)

    @pl.loop(0, n_part)
    def _(q):
        for k in range(2):
            part_copy(k, q).wait_send()
        for d in range(1, 4):
            hidden_copy(d, q).wait_send()


def per_device(
    tokens, slot_ids, gate_weights, old_expert, new_expert, gate_proj, up_proj, down_proj
):
    n_ep = lax.axis_size("ep")
    n_xy = n_ep // NZ
    tok, width = tokens.shape
    top = slot_ids.shape[1]
    slots, depth, block = gate_proj.shape
    cap = min(tok, (tok * top * 5 + 4 * n_ep - 1) // (4 * n_ep))
    slot_index = jnp.arange(slots, dtype=jnp.int32)
    holders = new_expert[:, None] == old_expert[None, :]
    source = jnp.min(jnp.where(holders, slot_index[None, :], slots - 1), axis=1).astype(jnp.int32)
    line_rows = NZ * cap
    n_rows = n_xy * line_rows
    n_part = 4
    dma = pltpu.SemaphoreType.DMA
    scratch = [
        pltpu.VMEM((slots, depth, block), BF16),
        pltpu.VMEM((slots, depth, block), BF16),
        pltpu.VMEM((slots, depth, block), BF16),
        pltpu.VMEM((3, slots, depth, block), BF16),
        pltpu.VMEM((2, 2, n_ep // 2, depth, block), BF16),
        pltpu.VMEM((4, n_ep // 4, depth, block), BF16),
        pltpu.VMEM((NZ, 2 * n_xy, tok), F32),
        pltpu.VMEM((NZ, 2 * n_xy, tok), F32),
        pltpu.VMEM((NZ, tok, width), BF16),
        pltpu.VMEM((line_rows, NZ * tok), BF16),
        pltpu.VMEM((NZ, tok, n_rows), BF16),
        pltpu.VMEM((n_xy, line_rows, width), BF16),
        pltpu.VMEM((2, n_xy, line_rows, width), BF16),
        pltpu.VMEM((2, n_rows, block), BF16),
        pltpu.VMEM((2, n_rows, block), BF16),
        pltpu.VMEM((2, n_rows, block), F32),
        pltpu.VMEM((4, n_rows, block), BF16),
        pltpu.VMEM((n_xy, line_rows, width), BF16),
        pltpu.VMEM((n_xy, line_rows, width), BF16),
        pltpu.VMEM((NZ, tok, width), BF16),
        pltpu.VMEM((NZ, tok, width), BF16),
        dma((4,)), dma((3,)), dma((3,)), dma((1,)), dma((NZ,)), dma((NZ,)), dma((NZ,)), dma((NZ,)),
        dma((n_xy,)), dma((n_xy,)), dma((n_xy,)), dma((n_xy,)), dma((2, n_part)), dma((2, n_part)),
        dma((4, n_part)), dma((4, n_part)), dma((n_xy,)), dma((n_xy,)), dma((NZ,)), dma((NZ,)),
    ]
    vmem = pl.BlockSpec(memory_space=pltpu.VMEM)
    hbm = pl.BlockSpec(memory_space=pl.ANY)
    return pl.pallas_call(
        functools.partial(layer_kernel, cap),
        out_shape=jax.ShapeDtypeStruct((tok, width), BF16),
        in_specs=[pl.BlockSpec(memory_space=pltpu.SMEM), hbm, vmem, vmem, hbm, hbm, hbm],
        out_specs=vmem,
        scratch_shapes=scratch,
        compiler_params=pltpu.CompilerParams(
            collective_id=0, has_side_effects=True, vmem_limit_bytes=60 * 1024 * 1024
        ),
        name="moe_layer",
    )(source, tokens, slot_ids.T, gate_weights.T, gate_proj, up_proj, down_proj)


def solution(mesh):
    placed = (
        P("ep", "et"), P("ep", None), P("ep", None), P(), P(),
        P(None, "ep", "et"), P(None, "ep", "et"), P(None, "ep", "et"),
    )
    return jax.shard_map(
        per_device, mesh=mesh, in_specs=placed, out_specs=P("ep", "et"), check_vma=False
    )
```

```python
import functools

import jax
import jax.numpy as jnp
from jax import lax
from jax.experimental import pallas as pl
from jax.experimental.pallas import tpu as pltpu
from jax.sharding import PartitionSpec as P

MESH = pl.DeviceIdType.MESH
NZ = 8
EARLY = 0
LATE = 0
F32 = jnp.float32
BF16 = jnp.bfloat16


def layer_kernel(
    cap, features,
    source_ref, tokens_hbm, slot_t_ref, gate_t_ref, gate_hbm, up_hbm, down_hbm, out_ref,
    stage_gate, stage_up, stage_down, wsend, gu_recv, down_recv, idx_send, idx_recv, tok_all, pick, combine,
    row_send, rows_in, hid, out_send, ret, ring_send, ring_recv,
    load_sem, wsend_sem, wrecv_sem, tok_send_sem, tok_recv_sem, idx_send_sem, idx_recv_sem,
    row_send_sem, row_recv_sem, fwd_send_sem, fwd_recv_sem,
    hid_send_sem, hid_recv_sem, out_send_sem, ret_recv_sem, ring_send_sem, ring_recv_sem,
):
    n_ep = stage_gate.shape[0]
    n_xy = n_ep // NZ
    tok = tok_all.shape[1]
    width = tok_all.shape[2]
    line_rows = NZ * cap
    n_rows = n_xy * line_rows
    ep = lax.axis_index("ep")
    et = lax.axis_index("et")
    me_xy, me_z = ep // NZ, ep % NZ
    h, c = et // 2, et % 2
    x_half = me_xy // (n_xy // 2)
    sibling = et + 1 - 2 * c
    across = (et + 2) % 4
    quarter = ep // (n_ep // 4)
    weights_hbm = (gate_hbm, up_hbm, down_hbm)
    stage = (stage_gate, stage_up, stage_down)

    loads = [
        pltpu.make_async_copy(weights_hbm[k], stage[k], load_sem.at[k]) for k in range(3)
    ]
    token_load = pltpu.make_async_copy(tokens_hbm, tok_all.at[me_z], load_sem.at[3])
    token_load.start()
    for load in loads:
        load.start()

    barrier = pltpu.get_barrier_semaphore()

    def greet(other_ep, other_et):
        pl.semaphore_signal(barrier, inc=1, device_id=(other_ep, other_et), device_id_type=MESH)

    @pl.loop(1, n_ep)
    def _(k):
        greet((ep + k) % n_ep, et)

    @pl.loop(0, n_ep)
    def _(k):
        other_ep, other_et = et * (n_ep // 4) + k // 4, k % 4

        @pl.when(jnp.logical_or(other_ep != ep, other_et != et))
        def _():
            greet(other_ep, other_et)

    for v in range(n_xy // 2):
        greet(((1 - x_half) * (n_xy // 2) + v) * NZ + me_z, across)
    for d in range(1, 4):
        greet(ep, (et + d) % 4)

    row = lax.broadcasted_iota(jnp.int32, (n_ep, tok), 0)
    row_slot = (row % n_xy) * NZ + row // n_xy
    named = jnp.zeros((n_ep, tok), F32)
    weight = jnp.zeros((n_ep, tok), F32)
    for k in range(slot_t_ref.shape[0]):
        hit = slot_t_ref[k : k + 1, :] == row_slot
        named = jnp.where(hit, 1.0, named)
        weight = jnp.where(hit, gate_t_ref[k : k + 1, :], weight)
    earlier = (
        lax.broadcasted_iota(jnp.int32, (tok, tok), 0) < lax.broadcasted_iota(jnp.int32, (tok, tok), 1)
    )
    place = jnp.dot(
        named.astype(BF16), jnp.where(earlier, 1.0, 0.0).astype(BF16), preferred_element_type=F32
    )
    place = jnp.where(named > 0.5, place, -100000.0)
    for z in range(NZ):
        idx_send[z, 0:n_xy, :] = place[z * n_xy : (z + 1) * n_xy]
        idx_send[z, n_xy : 2 * n_xy, :] = weight[z * n_xy : (z + 1) * n_xy]
    idx_recv[me_z] = idx_send[me_z]
    token_load.wait()

    same_down = jnp.where(quarter == et, 1, 0)
    pl.semaphore_wait(barrier, (n_ep - 1) + (n_ep - same_down) + n_xy // 2 + 3)

    half_tok = tok // 2
    far = NZ // 2

    def token_copy(way, s):
        owner = (me_z - way * (s - 1)) % NZ
        start, size = (0, tok) if s < far else ((0, half_tok) if way > 0 else (half_tok, half_tok))
        side = 0 if way > 0 else 1
        rows = tok_all.at[owner, pl.ds(start, size)]
        return pltpu.make_async_remote_copy(
            rows, rows, tok_send_sem.at[side, s], tok_recv_sem.at[side, s],
            device_id=(me_xy * NZ + (me_z + way) % NZ, et), device_id_type=MESH,
        )

    def index_copy(d):
        peer_z = (me_z + d) % NZ
        return pltpu.make_async_remote_copy(
            idx_send.at[peer_z], idx_recv.at[me_z], idx_send_sem.at[d], idx_recv_sem.at[d],
            device_id=(me_xy * NZ + peer_z, et), device_id_type=MESH,
        )

    for way in (1, -1):
        token_copy(way, 1).start()
    for d in range(1, NZ):
        index_copy(d).start()

    def weight_target(k):
        if k < 2:
            return et, gu_recv.at[k, ep]
        return quarter, down_recv.at[et, ep % (n_ep // 4)]

    def send_weights(k, first, last):
        target_et, target = weight_target(k)

        @pl.loop(first, last)
        def _(m):
            far_m = m - n_xy
            d_xy = jnp.where(m < n_xy, m, far_m % n_xy)
            d_z = jnp.where(m < n_xy, 0, 1 + far_m % (NZ - 1))
            slot = ((me_xy + d_xy) % n_xy) * NZ + (me_z + d_z) % NZ
            wsend[k, slot] = stage[k][source_ref[slot]]

            @pl.when(jnp.logical_or(slot != ep, target_et != et))
            def _():
                pltpu.make_async_remote_copy(
                    wsend.at[k, slot], target, wsend_sem.at[k], wrecv_sem.at[k],
                    device_id=(slot, target_et), device_id_type=MESH,
                ).start()

            @pl.when(jnp.logical_and(slot == ep, target_et == et))
            def _():
                pltpu.make_async_copy(wsend.at[k, slot], target, wrecv_sem.at[k]).start()

    def wait_weights(k):
        landed = gu_recv.at[k] if k < 2 else down_recv
        pltpu.make_async_copy(landed, landed, wrecv_sem.at[k]).wait()

    def wait_weights_sent(k):
        target_et, target = weight_target(k)

        @pl.loop(0, n_ep)
        def _(slot):
            @pl.when(jnp.logical_or(slot != ep, target_et != et))
            def _():
                pltpu.make_async_remote_copy(
                    wsend.at[k, slot], target, wsend_sem.at[k], wrecv_sem.at[k],
                    device_id=(slot, target_et), device_id_type=MESH,
                ).wait_send()

    low = 16
    rest = cap - low
    low_rows, rest_rows = NZ * low, NZ * rest
    row_low = lax.broadcasted_iota(jnp.int32, (low, tok), 0).astype(F32)
    row_rest = lax.broadcasted_iota(jnp.int32, (rest_rows, tok), 0).astype(F32)

    def low_part(z):
        places = idx_recv[z]
        picked = jnp.concatenate(
            [jnp.where(places[j : j + 1, :] == row_low, 1.0, 0.0) for j in range(n_xy)], axis=0
        ).astype(BF16)
        rows = jnp.dot(picked, tok_all[z], preferred_element_type=F32).astype(BF16)
        where = pl.ds(pl.multiple_of(z * low, low), low)
        for j in range(n_xy):
            row_send[j, where] = rows[j * low : (j + 1) * low]

    def rest_part():
        for z in range(NZ):
            places = idx_recv[z]
            at = jnp.where(places >= float(low), places + float(z * rest - low), -1.0)
            pick[:, z * tok : (z + 1) * tok] = jnp.concatenate(
                [jnp.where(at[j : j + 1, :] == row_rest, 1.0, 0.0) for j in range(n_xy)], axis=0
            ).astype(BF16)
        rows = jnp.dot(
            pick[...], tok_all[...].reshape(NZ * tok, width), preferred_element_type=F32
        ).astype(BF16)
        for j in range(n_xy):
            row_send[j, low_rows:line_rows] = rows[j * rest_rows : (j + 1) * rest_rows]

    for k in range(3):
        loads[k].wait()
        send_weights(k, 0, n_xy)
    send_weights(0, n_xy, n_xy + EARLY)
    low_part(me_z)
    for d in range(1, NZ):
        index_copy(d).wait_recv()
    for s in range(1, far + 1):
        for way in (1, -1):
            token_copy(way, s).wait_recv()
            if s < far:
                token_copy(way, s + 1).start()
        if s < far:
            send_weights(0, n_xy + s * EARLY, n_xy + (s + 1) * EARLY)
            low_part((me_z - s) % NZ)
            low_part((me_z + s) % NZ)
        else:
            send_weights(0, n_xy + far * EARLY, n_xy + far * EARLY + LATE)
            low_part((me_z + far) % NZ)
    rest_part()

    def row_copy(d):
        peer_xy = (me_xy + d) % n_xy
        same_x = x_half == peer_xy // (n_xy // 2)
        return pltpu.make_async_remote_copy(
            row_send.at[peer_xy], rows_in.at[et, me_xy], row_send_sem.at[d], row_recv_sem.at[d],
            device_id=(peer_xy * NZ + me_z, jnp.where(same_x, et, across)), device_id_type=MESH,
        )

    for d in range(1, n_xy):
        row_copy(d).start()
    rows_in[et, me_xy] = row_send[me_xy]
    send_weights(0, n_xy + far * EARLY + LATE, n_ep)

    send_weights(1, n_xy, n_ep)
    send_weights(2, n_xy, n_ep)

    def pass_copy(step, d):
        place_xy = (me_xy + n_xy - d) % n_xy
        same_x = x_half == place_xy // (n_xy // 2)
        near, other = jnp.where(same_x, et, across), jnp.where(same_x, across, et)
        rows = rows_in.at[other if step == 2 else near, place_xy]
        return pltpu.make_async_remote_copy(
            rows, rows, fwd_send_sem.at[step, d], fwd_recv_sem.at[step, d],
            device_id=(ep, across if step == 0 else sibling), device_id_type=MESH,
        )

    for d in range(n_xy):
        if d > 0:
            row_copy(d).wait_recv()
        pass_copy(0, d).start()
        pass_copy(1, d).start()

    lane = lax.broadcasted_iota(jnp.int32, (tok, 128), 1).astype(F32)

    @pl.loop(0, NZ)
    def _(z):
        table = idx_recv[z].T
        places, weights = table[:, 0:n_xy], table[:, n_xy : 2 * n_xy]
        at_rest = jnp.where(places >= float(low), places + (z * rest - low).astype(F32), -100000.0)
        at_low = jnp.where(places < float(low), places, -100000.0)
        per_tile = 128 // rest_rows
        total = jnp.zeros((tok, 128), F32)
        for j in range(n_xy):
            total = jnp.where(at_low[:, j : j + 1] + float(j * low) == lane, weights[:, j : j + 1], total)
        combine[z, :, 0:128] = total.astype(BF16)
        for tile in range(n_xy // per_tile):
            total = jnp.zeros((tok, 128), F32)
            for v in range(per_tile):
                j = tile * per_tile + v
                total = jnp.where(
                    at_rest[:, j : j + 1] + float(v * rest_rows) == lane, weights[:, j : j + 1], total
                )
            combine[z, :, (tile + 1) * 128 : (tile + 2) * 128] = total.astype(BF16)

    for d in range(n_xy):
        pass_copy(0, d).wait_recv()
        pass_copy(2, d).start()
    for d in range(n_xy):
        pass_copy(1, d).wait_recv()
        pass_copy(2, d).wait_recv()

    n_part = hid_send_sem.shape[1]
    part_rows = n_rows // n_part
    chunk_lines = n_xy // n_part
    block = hid.shape[2]

    def product(k, q):
        total = jnp.zeros((part_rows, block), F32)
        for v in range(4):
            left = rows_in[v, pl.ds(q * chunk_lines, chunk_lines)].reshape(part_rows, width)
            right = gu_recv[k, pl.ds(v * (n_ep // 4), n_ep // 4)].reshape(width, block)
            total = total + jnp.dot(left, right, preferred_element_type=F32)
        return total

    def hidden_copy(step, q):
        where = pl.ds(q * part_rows, part_rows)
        rows = hid.at[across if step == 2 else et, where]
        return pltpu.make_async_remote_copy(
            rows, rows, hid_send_sem.at[step, q], hid_recv_sem.at[step, q],
            device_id=(ep, across if step == 0 else sibling), device_id_type=MESH,
        )

    wait_weights(0)
    wait_weights(1)

    @pl.loop(0, n_part)
    def _(q):
        where = pl.ds(pl.multiple_of(q * part_rows, part_rows), part_rows)
        g = product(0, q)
        u = product(1, q)
        hid[et, where] = (g / (1.0 + jnp.exp(-g)) * u).astype(BF16)
        hidden_copy(0, q).start()
        hidden_copy(1, q).start()

    @pl.loop(0, n_part)
    def _(q):
        hidden_copy(0, q).wait_recv()
        hidden_copy(2, q).start()

    wait_weights(2)

    def out_copy(i, d, f):
        lanes = pl.ds(features[f][0], features[f][1])
        return pltpu.make_async_remote_copy(
            out_send.at[i, :, lanes], ret.at[me_xy, :, lanes], out_send_sem.at[d, f], ret_recv_sem.at[d, f],
            device_id=(i * NZ + me_z, et), device_id_type=MESH,
        )

    def down_chunk(q):
        hidden_copy(1, q).wait_recv()
        hidden_copy(2, q).wait_recv()
        where = pl.ds(pl.multiple_of(q * part_rows, part_rows), part_rows)
        total = jnp.zeros((part_rows, width), F32)
        for k in range(4):
            right = down_recv[k].reshape(width, block)
            total = total + lax.dot_general(
                hid[k, where], right, (((1,), (1,)), ((), ())), preferred_element_type=F32
            )
        total = total.astype(BF16)
        for v in range(chunk_lines):
            i = q * chunk_lines + v
            rows = total[v * line_rows : (v + 1) * line_rows]
            d = (i - me_xy + n_xy) % n_xy

            @pl.when(d == 0)
            def _():
                ret[me_xy] = rows

            @pl.when(d != 0)
            def _():
                out_send[i] = rows
                out_copy(i, d, 0).start()

    @pl.loop(0, n_part)
    def _(q):
        down_chunk(q)

    for f in range(1, len(features)):
        for d in range(1, n_xy):
            out_copy((me_xy + d) % n_xy, d, f).start()

    def line_sum(z, f):
        lanes = pl.ds(features[f][0], features[f][1])
        where = pl.ds(pl.multiple_of(z * low, low), low)
        near = ret[:, where, lanes].reshape(n_xy * low, features[f][1])
        others = ret[:, low_rows:line_rows, lanes].reshape(n_xy * rest_rows, features[f][1])
        total = jnp.dot(combine[z, :, 0:128], near, preferred_element_type=F32)
        return total + jnp.dot(combine[z, :, 128:], others, preferred_element_type=F32)

    def sum_copy(way, k, f):
        side = 0 if way > 0 else 1
        start, size = (0, tok) if k < far else ((0, half_tok) if way > 0 else (half_tok, half_tok))
        lanes = pl.ds(features[f][0], features[f][1])
        return pltpu.make_async_remote_copy(
            ring_send.at[side, k - 1, pl.ds(start, size), lanes],
            ring_recv.at[side, k - 1, pl.ds(start, size), lanes],
            ring_send_sem.at[side, k - 1, f], ring_recv_sem.at[side, k - 1, f],
            device_id=(me_xy * NZ + (me_z + way) % NZ, et), device_id_type=MESH,
        )

    def ring_step(k, f):
        lanes = pl.ds(features[f][0], features[f][1])
        if k == far:
            if f == 0 or len(features) > 1:
                for d in range(1, n_xy):
                    out_copy((me_xy + d) % n_xy, d, f).wait_recv()
            total = line_sum((me_z + far) % NZ, f).astype(BF16)
            for side, way in ((0, 1), (1, -1)):
                start = side * half_tok
                ring_send[side, k - 1, start : start + half_tok, lanes] = total[start : start + half_tok]
                sum_copy(way, k, f).start()
            return
        for side, way in ((0, 1), (1, -1)):
            total = line_sum((me_z + way * k) % NZ, f)
            sum_copy(way, k + 1, f).wait_recv()
            if k + 1 == far:
                start = side * half_tok
                other = half_tok - start
                ring_send[side, k - 1, start : start + half_tok, lanes] = (
                    total[start : start + half_tok]
                    + ring_recv[side, k, start : start + half_tok, lanes].astype(F32)
                ).astype(BF16)
                ring_send[side, k - 1, other : other + half_tok, lanes] = total[
                    other : other + half_tok
                ].astype(BF16)
            else:
                ring_send[side, k - 1, :, lanes] = (
                    total + ring_recv[side, k, :, lanes].astype(F32)
                ).astype(BF16)
            sum_copy(way, k, f).start()

    def finish(f):
        lanes = pl.ds(features[f][0], features[f][1])
        total = line_sum(me_z, f)
        for side, way in ((0, 1), (1, -1)):
            sum_copy(way, 1, f).wait_recv()
            total = total + ring_recv[side, 0, :, lanes].astype(F32)
        out_ref[:, lanes] = total.astype(BF16)

    lag = 2
    for t in range(far + lag * (len(features) - 1) + 1):
        for f in range(len(features)):
            s = t - lag * f
            if 0 <= s < far:
                ring_step(far - s, f)
            elif s == far:
                finish(f)

    for d in range(1, NZ):
        index_copy(d).wait_send()
    for way in (1, -1):
        for s in range(1, far + 1):
            token_copy(way, s).wait_send()
            for f in range(len(features)):
                sum_copy(way, s, f).wait_send()
    for d in range(1, n_xy):
        row_copy(d).wait_send()
        for f in range(len(features)):
            out_copy((me_xy + d) % n_xy, d, f).wait_send()
    for d in range(n_xy):
        for step in range(3):
            pass_copy(step, d).wait_send()
    for k in range(3):
        wait_weights_sent(k)

    @pl.loop(0, n_part)
    def _(q):
        for step in range(3):
            hidden_copy(step, q).wait_send()


def per_device(
    tokens, slot_ids, gate_weights, old_expert, new_expert, gate_proj, up_proj, down_proj
):
    n_ep = lax.axis_size("ep")
    n_xy = n_ep // NZ
    tok, width = tokens.shape
    top = slot_ids.shape[1]
    slots, depth, block = gate_proj.shape
    cap = min(tok, (tok * top * 5 + 4 * n_ep - 1) // (4 * n_ep))
    slot_index = jnp.arange(slots, dtype=jnp.int32)
    holders = new_expert[:, None] == old_expert[None, :]
    source = jnp.min(jnp.where(holders, slot_index[None, :], slots - 1), axis=1).astype(jnp.int32)
    line_rows = NZ * cap
    n_rows = n_xy * line_rows
    n_part = 4
    features = ((0, 512), (512, width - 512))
    n_feat = len(features)
    dma = pltpu.SemaphoreType.DMA
    scratch = [
        pltpu.VMEM((slots, depth, block), BF16),
        pltpu.VMEM((slots, depth, block), BF16),
        pltpu.VMEM((slots, depth, block), BF16),
        pltpu.VMEM((3, slots, depth, block), BF16),
        pltpu.VMEM((2, n_ep, depth, block), BF16),
        pltpu.VMEM((4, n_ep // 4, depth, block), BF16),
        pltpu.VMEM((NZ, 2 * n_xy, tok), F32),
        pltpu.VMEM((NZ, 2 * n_xy, tok), F32),
        pltpu.VMEM((NZ, tok, width), BF16),
        pltpu.VMEM((n_xy * NZ * (cap - 16), NZ * tok), BF16),
        pltpu.VMEM((NZ, tok, n_xy * (16 + NZ * (cap - 16))), BF16),
        pltpu.VMEM((n_xy, line_rows, width), BF16),
        pltpu.VMEM((4, n_xy, line_rows, width), BF16),
        pltpu.VMEM((4, n_rows, block), BF16),
        pltpu.VMEM((n_xy, line_rows, width), BF16),
        pltpu.VMEM((n_xy, line_rows, width), BF16),
        pltpu.VMEM((2, NZ // 2, tok, width), BF16),
        pltpu.VMEM((2, NZ // 2, tok, width), BF16),
        dma((4,)), dma((3,)), dma((3,)), dma((2, NZ // 2 + 1)), dma((2, NZ // 2 + 1)), dma((NZ,)), dma((NZ,)),
        dma((n_xy,)), dma((n_xy,)), dma((3, n_xy)), dma((3, n_xy)),
        dma((3, n_part)), dma((3, n_part)), dma((n_xy, n_feat)), dma((n_xy, n_feat)),
        dma((2, NZ // 2, n_feat)), dma((2, NZ // 2, n_feat)),
    ]
    vmem = pl.BlockSpec(memory_space=pltpu.VMEM)
    hbm = pl.BlockSpec(memory_space=pl.ANY)
    return pl.pallas_call(
        functools.partial(layer_kernel, cap, features),
        out_shape=jax.ShapeDtypeStruct((tok, width), BF16),
        in_specs=[pl.BlockSpec(memory_space=pltpu.SMEM), hbm, vmem, vmem, hbm, hbm, hbm],
        out_specs=vmem,
        scratch_shapes=scratch,
        compiler_params=pltpu.CompilerParams(
            collective_id=0, has_side_effects=True, vmem_limit_bytes=60 * 1024 * 1024
        ),
        name="moe_layer",
    )(source, tokens, slot_ids.T, gate_weights.T, gate_proj, up_proj, down_proj)


def solution(mesh):
    placed = (
        P("ep", "et"), P("ep", None), P("ep", None), P(), P(),
        P(None, "ep", "et"), P(None, "ep", "et"), P(None, "ep", "et"),
    )
    return jax.shard_map(
        per_device, mesh=mesh, in_specs=placed, out_specs=P("ep", "et"), check_vma=False
    )
```

```python
import functools

import jax
import jax.numpy as jnp
from jax import lax
from jax.experimental import pallas as pl
from jax.experimental.pallas import tpu as pltpu
from jax.sharding import PartitionSpec as P

MESH = pl.DeviceIdType.MESH
NZ = 8
EARLY = 24
F32 = jnp.float32
BF16 = jnp.bfloat16


def layer_kernel(
    cap, features,
    source_ref, tokens_hbm, slot_t_ref, gate_t_ref, gate_hbm, up_hbm, down_hbm, out_ref,
    stage_gate, stage_up, stage_down, wsend, gu_recv, down_recv, idx_send, idx_recv, tok_all, pick, combine,
    row_send, rows_in, hid, out_send, ret, ring_send, ring_recv,
    load_sem, wsend_sem, wrecv_sem, tok_send_sem, tok_recv_sem, idx_send_sem, idx_recv_sem,
    row_send_sem, row_recv_sem, fwd_send_sem, fwd_recv_sem,
    hid_send_sem, hid_recv_sem, out_send_sem, ret_recv_sem, ring_send_sem, ring_recv_sem,
):
    n_ep = stage_gate.shape[0]
    n_xy = n_ep // NZ
    tok = tok_all.shape[1]
    width = tok_all.shape[2]
    line_rows = NZ * cap
    n_rows = n_xy * line_rows
    ep = lax.axis_index("ep")
    et = lax.axis_index("et")
    me_xy, me_z = ep // NZ, ep % NZ
    h, c = et // 2, et % 2
    x_half = me_xy // (n_xy // 2)
    sibling = et + 1 - 2 * c
    across = (et + 2) % 4
    quarter = ep // (n_ep // 4)
    weights_hbm = (gate_hbm, up_hbm, down_hbm)
    stage = (stage_gate, stage_up, stage_down)

    loads = [
        pltpu.make_async_copy(weights_hbm[k], stage[k], load_sem.at[k]) for k in range(3)
    ]
    token_load = pltpu.make_async_copy(tokens_hbm, tok_all.at[me_z], load_sem.at[3])
    token_load.start()
    for load in loads:
        load.start()

    barrier = pltpu.get_barrier_semaphore()

    def greet(other_ep, other_et):
        pl.semaphore_signal(barrier, inc=1, device_id=(other_ep, other_et), device_id_type=MESH)

    @pl.loop(1, n_ep)
    def _(k):
        greet((ep + k) % n_ep, et)

    @pl.loop(0, n_ep)
    def _(k):
        other_ep, other_et = et * (n_ep // 4) + k // 4, k % 4

        @pl.when(jnp.logical_or(other_ep != ep, other_et != et))
        def _():
            greet(other_ep, other_et)

    for v in range(n_xy // 2):
        greet(((1 - x_half) * (n_xy // 2) + v) * NZ + me_z, across)
    for d in range(1, 4):
        greet(ep, (et + d) % 4)

    row = lax.broadcasted_iota(jnp.int32, (n_ep, tok), 0)
    row_slot = (row % n_xy) * NZ + row // n_xy
    named = jnp.zeros((n_ep, tok), F32)
    weight = jnp.zeros((n_ep, tok), F32)
    for k in range(slot_t_ref.shape[0]):
        hit = slot_t_ref[k : k + 1, :] == row_slot
        named = jnp.where(hit, 1.0, named)
        weight = jnp.where(hit, gate_t_ref[k : k + 1, :], weight)
    earlier = (
        lax.broadcasted_iota(jnp.int32, (tok, tok), 0) < lax.broadcasted_iota(jnp.int32, (tok, tok), 1)
    )
    place = jnp.dot(
        named.astype(BF16), jnp.where(earlier, 1.0, 0.0).astype(BF16), preferred_element_type=F32
    )
    place = jnp.where(named > 0.5, place, -100000.0)
    for z in range(NZ):
        idx_send[z, 0:n_xy, :] = place[z * n_xy : (z + 1) * n_xy]
        idx_send[z, n_xy : 2 * n_xy, :] = weight[z * n_xy : (z + 1) * n_xy]
    idx_recv[me_z] = idx_send[me_z]
    token_load.wait()

    same_down = jnp.where(quarter == et, 1, 0)
    pl.semaphore_wait(barrier, (n_ep - 1) + (n_ep - same_down) + n_xy // 2 + 3)

    half_tok = tok // 2
    far = NZ // 2

    def token_copy(way, s):
        owner = (me_z - way * (s - 1)) % NZ
        start, size = (0, tok) if s < far else ((0, half_tok) if way > 0 else (half_tok, half_tok))
        side = 0 if way > 0 else 1
        rows = tok_all.at[owner, pl.ds(start, size)]
        return pltpu.make_async_remote_copy(
            rows, rows, tok_send_sem.at[side, s], tok_recv_sem.at[side, s],
            device_id=(me_xy * NZ + (me_z + way) % NZ, et), device_id_type=MESH,
        )

    def index_copy(d):
        peer_z = (me_z + d) % NZ
        return pltpu.make_async_remote_copy(
            idx_send.at[peer_z], idx_recv.at[me_z], idx_send_sem.at[d], idx_recv_sem.at[d],
            device_id=(me_xy * NZ + peer_z, et), device_id_type=MESH,
        )

    for way in (1, -1):
        token_copy(way, 1).start()
    for d in range(1, NZ):
        index_copy(d).start()

    def weight_target(k):
        if k < 2:
            return et, gu_recv.at[k, ep]
        return quarter, down_recv.at[et, ep % (n_ep // 4)]

    def send_weights(k, first, last):
        target_et, target = weight_target(k)

        @pl.loop(first, last)
        def _(m):
            far_m = m - n_xy
            d_xy = jnp.where(m < n_xy, m, far_m % n_xy)
            d_z = jnp.where(m < n_xy, 0, 1 + far_m % (NZ - 1))
            slot = ((me_xy + d_xy) % n_xy) * NZ + (me_z + d_z) % NZ
            wsend[k, slot] = stage[k][source_ref[slot]]

            @pl.when(jnp.logical_or(slot != ep, target_et != et))
            def _():
                pltpu.make_async_remote_copy(
                    wsend.at[k, slot], target, wsend_sem.at[k], wrecv_sem.at[k],
                    device_id=(slot, target_et), device_id_type=MESH,
                ).start()

            @pl.when(jnp.logical_and(slot == ep, target_et == et))
            def _():
                pltpu.make_async_copy(wsend.at[k, slot], target, wrecv_sem.at[k]).start()

    def wait_weights(k):
        landed = gu_recv.at[k] if k < 2 else down_recv
        pltpu.make_async_copy(landed, landed, wrecv_sem.at[k]).wait()

    def wait_weights_sent(k):
        target_et, target = weight_target(k)

        @pl.loop(0, n_ep)
        def _(slot):
            @pl.when(jnp.logical_or(slot != ep, target_et != et))
            def _():
                pltpu.make_async_remote_copy(
                    wsend.at[k, slot], target, wsend_sem.at[k], wrecv_sem.at[k],
                    device_id=(slot, target_et), device_id_type=MESH,
                ).wait_send()

    low = 16
    rest = cap - low
    low_rows, rest_rows = NZ * low, NZ * rest
    row_low = lax.broadcasted_iota(jnp.int32, (low, tok), 0).astype(F32)
    row_rest = lax.broadcasted_iota(jnp.int32, (rest_rows, tok), 0).astype(F32)

    def low_part(z):
        places = idx_recv[z]
        picked = jnp.concatenate(
            [jnp.where(places[j : j + 1, :] == row_low, 1.0, 0.0) for j in range(n_xy)], axis=0
        ).astype(BF16)
        rows = jnp.dot(picked, tok_all[z], preferred_element_type=F32).astype(BF16)
        where = pl.ds(pl.multiple_of(z * low, low), low)
        for j in range(n_xy):
            row_send[j, where] = rows[j * low : (j + 1) * low]

    def rest_part():
        for z in range(NZ):
            places = idx_recv[z]
            at = jnp.where(places >= float(low), places + float(z * rest - low), -1.0)
            pick[:, z * tok : (z + 1) * tok] = jnp.concatenate(
                [jnp.where(at[j : j + 1, :] == row_rest, 1.0, 0.0) for j in range(n_xy)], axis=0
            ).astype(BF16)
        rows = jnp.dot(
            pick[...], tok_all[...].reshape(NZ * tok, width), preferred_element_type=F32
        ).astype(BF16)
        for j in range(n_xy):
            row_send[j, low_rows:line_rows] = rows[j * rest_rows : (j + 1) * rest_rows]

    for k in range(3):
        loads[k].wait()
        send_weights(k, 0, n_xy)
    low_part(me_z)
    for d in range(1, NZ):
        index_copy(d).wait_recv()
    for s in range(1, far + 1):
        for way in (1, -1):
            token_copy(way, s).wait_recv()
            if s < far:
                token_copy(way, s + 1).start()
        if s == far - 1:
            send_weights(0, n_xy, n_xy + EARLY)
        low_part((me_z + s) % NZ)
        if s < far:
            low_part((me_z - s) % NZ)
    rest_part()

    def row_copy(d):
        peer_xy = (me_xy + d) % n_xy
        same_x = x_half == peer_xy // (n_xy // 2)
        return pltpu.make_async_remote_copy(
            row_send.at[peer_xy], rows_in.at[et, me_xy], row_send_sem.at[d], row_recv_sem.at[d],
            device_id=(peer_xy * NZ + me_z, jnp.where(same_x, et, across)), device_id_type=MESH,
        )

    for d in range(1, n_xy):
        row_copy(d).start()
    rows_in[et, me_xy] = row_send[me_xy]
    send_weights(0, n_xy + EARLY, n_ep)

    send_weights(1, n_xy, n_ep)
    send_weights(2, n_xy, n_ep)

    def pass_copy(step, d):
        place_xy = (me_xy + n_xy - d) % n_xy
        same_x = x_half == place_xy // (n_xy // 2)
        near, other = jnp.where(same_x, et, across), jnp.where(same_x, across, et)
        rows = rows_in.at[other if step == 2 else near, place_xy]
        return pltpu.make_async_remote_copy(
            rows, rows, fwd_send_sem.at[step, d], fwd_recv_sem.at[step, d],
            device_id=(ep, across if step == 0 else sibling), device_id_type=MESH,
        )

    for d in range(n_xy):
        if d > 0:
            row_copy(d).wait_recv()
        pass_copy(0, d).start()
        pass_copy(1, d).start()

    lane = lax.broadcasted_iota(jnp.int32, (tok, 128), 1).astype(F32)

    @pl.loop(0, NZ)
    def _(z):
        table = idx_recv[z].T
        places, weights = table[:, 0:n_xy], table[:, n_xy : 2 * n_xy]
        at_rest = jnp.where(places >= float(low), places + (z * rest - low).astype(F32), -100000.0)
        at_low = jnp.where(places < float(low), places, -100000.0)
        per_tile = 128 // rest_rows
        total = jnp.zeros((tok, 128), F32)
        for j in range(n_xy):
            total = jnp.where(at_low[:, j : j + 1] + float(j * low) == lane, weights[:, j : j + 1], total)
        combine[z, :, 0:128] = total.astype(BF16)
        for tile in range(n_xy // per_tile):
            total = jnp.zeros((tok, 128), F32)
            for v in range(per_tile):
                j = tile * per_tile + v
                total = jnp.where(
                    at_rest[:, j : j + 1] + float(v * rest_rows) == lane, weights[:, j : j + 1], total
                )
            combine[z, :, (tile + 1) * 128 : (tile + 2) * 128] = total.astype(BF16)

    for d in range(n_xy):
        pass_copy(0, d).wait_recv()
        pass_copy(2, d).start()
    for d in range(n_xy):
        pass_copy(1, d).wait_recv()
        pass_copy(2, d).wait_recv()

    n_part = hid_send_sem.shape[1]
    part_rows = n_rows // n_part
    chunk_lines = n_xy // n_part
    block = hid.shape[2]

    def product(k, q):
        total = jnp.zeros((part_rows, block), F32)
        for v in range(4):
            left = rows_in[v, pl.ds(q * chunk_lines, chunk_lines)].reshape(part_rows, width)
            right = gu_recv[k, pl.ds(v * (n_ep // 4), n_ep // 4)].reshape(width, block)
            total = total + jnp.dot(left, right, preferred_element_type=F32)
        return total

    def hidden_copy(step, q):
        where = pl.ds(q * part_rows, part_rows)
        rows = hid.at[across if step == 2 else et, where]
        return pltpu.make_async_remote_copy(
            rows, rows, hid_send_sem.at[step, q], hid_recv_sem.at[step, q],
            device_id=(ep, across if step == 0 else sibling), device_id_type=MESH,
        )

    wait_weights(0)
    wait_weights(1)

    @pl.loop(0, n_part)
    def _(q):
        where = pl.ds(pl.multiple_of(q * part_rows, part_rows), part_rows)
        g = product(0, q)
        u = product(1, q)
        hid[et, where] = (g / (1.0 + jnp.exp(-g)) * u).astype(BF16)
        hidden_copy(0, q).start()
        hidden_copy(1, q).start()

    @pl.loop(0, n_part)
    def _(q):
        hidden_copy(0, q).wait_recv()
        hidden_copy(2, q).start()

    wait_weights(2)

    def out_copy(i, d, f):
        lanes = pl.ds(features[f][0], features[f][1])
        return pltpu.make_async_remote_copy(
            out_send.at[i, :, lanes], ret.at[me_xy, :, lanes], out_send_sem.at[d, f], ret_recv_sem.at[d, f],
            device_id=(i * NZ + me_z, et), device_id_type=MESH,
        )

    def down_chunk(q):
        hidden_copy(1, q).wait_recv()
        hidden_copy(2, q).wait_recv()
        where = pl.ds(pl.multiple_of(q * part_rows, part_rows), part_rows)
        total = jnp.zeros((part_rows, width), F32)
        for k in range(4):
            right = down_recv[k].reshape(width, block)
            total = total + lax.dot_general(
                hid[k, where], right, (((1,), (1,)), ((), ())), preferred_element_type=F32
            )
        total = total.astype(BF16)
        for v in range(chunk_lines):
            i = q * chunk_lines + v
            rows = total[v * line_rows : (v + 1) * line_rows]
            d = (i - me_xy + n_xy) % n_xy

            @pl.when(d == 0)
            def _():
                ret[me_xy] = rows

            @pl.when(d != 0)
            def _():
                out_send[i] = rows
                out_copy(i, d, 0).start()

    @pl.loop(0, n_part)
    def _(q):
        down_chunk(q)

    for f in range(1, len(features)):
        for d in range(1, n_xy):
            out_copy((me_xy + d) % n_xy, d, f).start()

    def line_sum(z, f):
        lanes = pl.ds(features[f][0], features[f][1])
        where = pl.ds(pl.multiple_of(z * low, low), low)
        near = ret[:, where, lanes].reshape(n_xy * low, features[f][1])
        others = ret[:, low_rows:line_rows, lanes].reshape(n_xy * rest_rows, features[f][1])
        total = jnp.dot(combine[z, :, 0:128], near, preferred_element_type=F32)
        return total + jnp.dot(combine[z, :, 128:], others, preferred_element_type=F32)

    def sum_copy(way, k, f):
        side = 0 if way > 0 else 1
        start, size = (0, tok) if k < far else ((0, half_tok) if way > 0 else (half_tok, half_tok))
        lanes = pl.ds(features[f][0], features[f][1])
        return pltpu.make_async_remote_copy(
            ring_send.at[side, k - 1, pl.ds(start, size), lanes],
            ring_recv.at[side, k - 1, pl.ds(start, size), lanes],
            ring_send_sem.at[side, k - 1, f], ring_recv_sem.at[side, k - 1, f],
            device_id=(me_xy * NZ + (me_z + way) % NZ, et), device_id_type=MESH,
        )

    def ring_step(k, f):
        lanes = pl.ds(features[f][0], features[f][1])
        if k == far:
            if f == 0 or len(features) > 1:
                for d in range(1, n_xy):
                    out_copy((me_xy + d) % n_xy, d, f).wait_recv()
            total = line_sum((me_z + far) % NZ, f).astype(BF16)
            for side, way in ((0, 1), (1, -1)):
                start = side * half_tok
                ring_send[side, k - 1, start : start + half_tok, lanes] = total[start : start + half_tok]
                sum_copy(way, k, f).start()
            return
        for side, way in ((0, 1), (1, -1)):
            total = line_sum((me_z + way * k) % NZ, f)
            sum_copy(way, k + 1, f).wait_recv()
            if k + 1 == far:
                start = side * half_tok
                other = half_tok - start
                ring_send[side, k - 1, start : start + half_tok, lanes] = (
                    total[start : start + half_tok]
                    + ring_recv[side, k, start : start + half_tok, lanes].astype(F32)
                ).astype(BF16)
                ring_send[side, k - 1, other : other + half_tok, lanes] = total[
                    other : other + half_tok
                ].astype(BF16)
            else:
                ring_send[side, k - 1, :, lanes] = (
                    total + ring_recv[side, k, :, lanes].astype(F32)
                ).astype(BF16)
            sum_copy(way, k, f).start()

    def finish(f):
        lanes = pl.ds(features[f][0], features[f][1])
        total = line_sum(me_z, f)
        for side, way in ((0, 1), (1, -1)):
            sum_copy(way, 1, f).wait_recv()
            total = total + ring_recv[side, 0, :, lanes].astype(F32)
        out_ref[:, lanes] = total.astype(BF16)

    lag = 2
    for t in range(far + lag * (len(features) - 1) + 1):
        for f in range(len(features)):
            s = t - lag * f
            if 0 <= s < far:
                ring_step(far - s, f)
            elif s == far:
                finish(f)

    for d in range(1, NZ):
        index_copy(d).wait_send()
    for way in (1, -1):
        for s in range(1, far + 1):
            token_copy(way, s).wait_send()
            for f in range(len(features)):
                sum_copy(way, s, f).wait_send()
    for d in range(1, n_xy):
        row_copy(d).wait_send()
        for f in range(len(features)):
            out_copy((me_xy + d) % n_xy, d, f).wait_send()
    for d in range(n_xy):
        for step in range(3):
            pass_copy(step, d).wait_send()
    for k in range(3):
        wait_weights_sent(k)

    @pl.loop(0, n_part)
    def _(q):
        for step in range(3):
            hidden_copy(step, q).wait_send()


def per_device(
    tokens, slot_ids, gate_weights, old_expert, new_expert, gate_proj, up_proj, down_proj
):
    n_ep = lax.axis_size("ep")
    n_xy = n_ep // NZ
    tok, width = tokens.shape
    top = slot_ids.shape[1]
    slots, depth, block = gate_proj.shape
    cap = min(tok, (tok * top * 5 + 4 * n_ep - 1) // (4 * n_ep))
    slot_index = jnp.arange(slots, dtype=jnp.int32)
    holders = new_expert[:, None] == old_expert[None, :]
    source = jnp.min(jnp.where(holders, slot_index[None, :], slots - 1), axis=1).astype(jnp.int32)
    line_rows = NZ * cap
    n_rows = n_xy * line_rows
    n_part = 4
    features = ((0, 512), (512, width - 512))
    n_feat = len(features)
    dma = pltpu.SemaphoreType.DMA
    scratch = [
        pltpu.VMEM((slots, depth, block), BF16),
        pltpu.VMEM((slots, depth, block), BF16),
        pltpu.VMEM((slots, depth, block), BF16),
        pltpu.VMEM((3, slots, depth, block), BF16),
        pltpu.VMEM((2, n_ep, depth, block), BF16),
        pltpu.VMEM((4, n_ep // 4, depth, block), BF16),
        pltpu.VMEM((NZ, 2 * n_xy, tok), F32),
        pltpu.VMEM((NZ, 2 * n_xy, tok), F32),
        pltpu.VMEM((NZ, tok, width), BF16),
        pltpu.VMEM((n_xy * NZ * (cap - 16), NZ * tok), BF16),
        pltpu.VMEM((NZ, tok, n_xy * (16 + NZ * (cap - 16))), BF16),
        pltpu.VMEM((n_xy, line_rows, width), BF16),
        pltpu.VMEM((4, n_xy, line_rows, width), BF16),
        pltpu.VMEM((4, n_rows, block), BF16),
        pltpu.VMEM((n_xy, line_rows, width), BF16),
        pltpu.VMEM((n_xy, line_rows, width), BF16),
        pltpu.VMEM((2, NZ // 2, tok, width), BF16),
        pltpu.VMEM((2, NZ // 2, tok, width), BF16),
        dma((4,)), dma((3,)), dma((3,)), dma((2, NZ // 2 + 1)), dma((2, NZ // 2 + 1)), dma((NZ,)), dma((NZ,)),
        dma((n_xy,)), dma((n_xy,)), dma((3, n_xy)), dma((3, n_xy)),
        dma((3, n_part)), dma((3, n_part)), dma((n_xy, n_feat)), dma((n_xy, n_feat)),
        dma((2, NZ // 2, n_feat)), dma((2, NZ // 2, n_feat)),
    ]
    vmem = pl.BlockSpec(memory_space=pltpu.VMEM)
    hbm = pl.BlockSpec(memory_space=pl.ANY)
    return pl.pallas_call(
        functools.partial(layer_kernel, cap, features),
        out_shape=jax.ShapeDtypeStruct((tok, width), BF16),
        in_specs=[pl.BlockSpec(memory_space=pltpu.SMEM), hbm, vmem, vmem, hbm, hbm, hbm],
        out_specs=vmem,
        scratch_shapes=scratch,
        compiler_params=pltpu.CompilerParams(
            collective_id=0, has_side_effects=True, vmem_limit_bytes=60 * 1024 * 1024
        ),
        name="moe_layer",
    )(source, tokens, slot_ids.T, gate_weights.T, gate_proj, up_proj, down_proj)


def solution(mesh):
    placed = (
        P("ep", "et"), P("ep", None), P("ep", None), P(), P(),
        P(None, "ep", "et"), P(None, "ep", "et"), P(None, "ep", "et"),
    )
    return jax.shard_map(
        per_device, mesh=mesh, in_specs=placed, out_specs=P("ep", "et"), check_vma=False
    )
```

```python
import functools

import jax
import jax.numpy as jnp
from jax import lax
from jax.experimental import pallas as pl
from jax.experimental.pallas import tpu as pltpu
from jax.sharding import PartitionSpec as P

MESH = pl.DeviceIdType.MESH
NZ = 8
EARLY = 24
F32 = jnp.float32
BF16 = jnp.bfloat16


def layer_kernel(
    cap, features,
    source_ref, tokens_hbm, slot_t_ref, gate_t_ref, gate_hbm, up_hbm, down_hbm, out_ref,
    stage_gate, stage_up, stage_down, wsend, gu_recv, down_recv, idx_send, idx_recv, tok_all, pick, combine,
    row_send, rows_in, hid, out_send, ret, rest_sum, ring_send, ring_recv,
    load_sem, wsend_sem, wrecv_sem, tok_send_sem, tok_recv_sem, idx_send_sem, idx_recv_sem,
    row_send_sem, row_recv_sem, fwd_send_sem, fwd_recv_sem,
    hid_send_sem, hid_recv_sem, out_send_sem, ret_recv_sem, ring_send_sem, ring_recv_sem,
):
    n_ep = stage_gate.shape[0]
    n_xy = n_ep // NZ
    tok = tok_all.shape[1]
    width = tok_all.shape[2]
    line_rows = NZ * cap
    n_rows = n_xy * line_rows
    ep = lax.axis_index("ep")
    et = lax.axis_index("et")
    me_xy, me_z = ep // NZ, ep % NZ
    h, c = et // 2, et % 2
    x_half = me_xy // (n_xy // 2)
    sibling = et + 1 - 2 * c
    across = (et + 2) % 4
    quarter = ep // (n_ep // 4)
    weights_hbm = (gate_hbm, up_hbm, down_hbm)
    stage = (stage_gate, stage_up, stage_down)

    loads = [
        pltpu.make_async_copy(weights_hbm[k], stage[k], load_sem.at[k]) for k in range(3)
    ]
    token_load = pltpu.make_async_copy(tokens_hbm, tok_all.at[me_z], load_sem.at[3])
    token_load.start()
    for load in loads:
        load.start()

    barrier = pltpu.get_barrier_semaphore()

    def greet(other_ep, other_et):
        pl.semaphore_signal(barrier, inc=1, device_id=(other_ep, other_et), device_id_type=MESH)

    @pl.loop(1, n_ep)
    def _(k):
        greet((ep + k) % n_ep, et)

    @pl.loop(0, n_ep)
    def _(k):
        other_ep, other_et = et * (n_ep // 4) + k // 4, k % 4

        @pl.when(jnp.logical_or(other_ep != ep, other_et != et))
        def _():
            greet(other_ep, other_et)

    for v in range(n_xy // 2):
        greet(((1 - x_half) * (n_xy // 2) + v) * NZ + me_z, across)
    for d in range(1, 4):
        greet(ep, (et + d) % 4)

    row = lax.broadcasted_iota(jnp.int32, (n_ep, tok), 0)
    row_slot = (row % n_xy) * NZ + row // n_xy
    named = jnp.zeros((n_ep, tok), F32)
    weight = jnp.zeros((n_ep, tok), F32)
    for k in range(slot_t_ref.shape[0]):
        hit = slot_t_ref[k : k + 1, :] == row_slot
        named = jnp.where(hit, 1.0, named)
        weight = jnp.where(hit, gate_t_ref[k : k + 1, :], weight)
    earlier = (
        lax.broadcasted_iota(jnp.int32, (tok, tok), 0) < lax.broadcasted_iota(jnp.int32, (tok, tok), 1)
    )
    place = jnp.dot(
        named.astype(BF16), jnp.where(earlier, 1.0, 0.0).astype(BF16), preferred_element_type=F32
    )
    place = jnp.where(named > 0.5, place, -100000.0)
    for z in range(NZ):
        idx_send[z, 0:n_xy, :] = place[z * n_xy : (z + 1) * n_xy]
        idx_send[z, n_xy : 2 * n_xy, :] = weight[z * n_xy : (z + 1) * n_xy]
    idx_recv[me_z] = idx_send[me_z]
    token_load.wait()

    same_down = jnp.where(quarter == et, 1, 0)
    pl.semaphore_wait(barrier, (n_ep - 1) + (n_ep - same_down) + n_xy // 2 + 3)

    half_tok = tok // 2
    far = NZ // 2

    def token_copy(way, s):
        owner = (me_z - way * (s - 1)) % NZ
        start, size = (0, tok) if s < far else ((0, half_tok) if way > 0 else (half_tok, half_tok))
        side = 0 if way > 0 else 1
        rows = tok_all.at[owner, pl.ds(start, size)]
        return pltpu.make_async_remote_copy(
            rows, rows, tok_send_sem.at[side, s], tok_recv_sem.at[side, s],
            device_id=(me_xy * NZ + (me_z + way) % NZ, et), device_id_type=MESH,
        )

    def index_copy(d):
        peer_z = (me_z + d) % NZ
        return pltpu.make_async_remote_copy(
            idx_send.at[peer_z], idx_recv.at[me_z], idx_send_sem.at[d], idx_recv_sem.at[d],
            device_id=(me_xy * NZ + peer_z, et), device_id_type=MESH,
        )

    for way in (1, -1):
        token_copy(way, 1).start()
    for d in range(1, NZ):
        index_copy(d).start()

    def weight_target(k):
        if k < 2:
            return et, gu_recv.at[k, ep]
        return quarter, down_recv.at[et, ep % (n_ep // 4)]

    def send_weights(k, first, last):
        target_et, target = weight_target(k)

        @pl.loop(first, last)
        def _(m):
            far_m = m - n_xy
            d_xy = jnp.where(m < n_xy, m, far_m % n_xy)
            d_z = jnp.where(m < n_xy, 0, 1 + far_m % (NZ - 1))
            slot = ((me_xy + d_xy) % n_xy) * NZ + (me_z + d_z) % NZ
            wsend[k, slot] = stage[k][source_ref[slot]]

            @pl.when(jnp.logical_or(slot != ep, target_et != et))
            def _():
                pltpu.make_async_remote_copy(
                    wsend.at[k, slot], target, wsend_sem.at[k], wrecv_sem.at[k],
                    device_id=(slot, target_et), device_id_type=MESH,
                ).start()

            @pl.when(jnp.logical_and(slot == ep, target_et == et))
            def _():
                pltpu.make_async_copy(wsend.at[k, slot], target, wrecv_sem.at[k]).start()

    def wait_weights(k):
        landed = gu_recv.at[k] if k < 2 else down_recv
        pltpu.make_async_copy(landed, landed, wrecv_sem.at[k]).wait()

    def wait_weights_sent(k):
        target_et, target = weight_target(k)

        @pl.loop(0, n_ep)
        def _(slot):
            @pl.when(jnp.logical_or(slot != ep, target_et != et))
            def _():
                pltpu.make_async_remote_copy(
                    wsend.at[k, slot], target, wsend_sem.at[k], wrecv_sem.at[k],
                    device_id=(slot, target_et), device_id_type=MESH,
                ).wait_send()

    low = 16
    rest = cap - low
    low_rows, rest_rows = NZ * low, NZ * rest
    row_low = lax.broadcasted_iota(jnp.int32, (low, tok), 0).astype(F32)
    row_rest = lax.broadcasted_iota(jnp.int32, (rest_rows, tok), 0).astype(F32)

    def low_part(z):
        places = idx_recv[z]
        picked = jnp.concatenate(
            [jnp.where(places[j : j + 1, :] == row_low, 1.0, 0.0) for j in range(n_xy)], axis=0
        ).astype(BF16)
        rows = jnp.dot(picked, tok_all[z], preferred_element_type=F32).astype(BF16)
        where = pl.ds(pl.multiple_of(z * low, low), low)
        for j in range(n_xy):
            row_send[j, where] = rows[j * low : (j + 1) * low]

    def rest_part():
        for z in range(NZ):
            places = idx_recv[z]
            at = jnp.where(places >= float(low), places + float(z * rest - low), -1.0)
            pick[:, z * tok : (z + 1) * tok] = jnp.concatenate(
                [jnp.where(at[j : j + 1, :] == row_rest, 1.0, 0.0) for j in range(n_xy)], axis=0
            ).astype(BF16)
        rows = jnp.dot(
            pick[...], tok_all[...].reshape(NZ * tok, width), preferred_element_type=F32
        ).astype(BF16)
        for j in range(n_xy):
            row_send[j, low_rows:line_rows] = rows[j * rest_rows : (j + 1) * rest_rows]

    for k in range(3):
        loads[k].wait()
        send_weights(k, 0, n_xy)
    low_part(me_z)
    for d in range(1, NZ):
        index_copy(d).wait_recv()
    for s in range(1, far + 1):
        for way in (1, -1):
            token_copy(way, s).wait_recv()
            if s < far:
                token_copy(way, s + 1).start()
        if s == far - 1:
            send_weights(0, n_xy, n_xy + EARLY)
        low_part((me_z + s) % NZ)
        if s < far:
            low_part((me_z - s) % NZ)
    rest_part()

    def row_copy(d):
        peer_xy = (me_xy + d) % n_xy
        same_x = x_half == peer_xy // (n_xy // 2)
        return pltpu.make_async_remote_copy(
            row_send.at[peer_xy], rows_in.at[et, me_xy], row_send_sem.at[d], row_recv_sem.at[d],
            device_id=(peer_xy * NZ + me_z, jnp.where(same_x, et, across)), device_id_type=MESH,
        )

    for d in range(1, n_xy):
        row_copy(d).start()
    rows_in[et, me_xy] = row_send[me_xy]
    send_weights(0, n_xy + EARLY, n_ep)

    send_weights(1, n_xy, n_ep)
    send_weights(2, n_xy, n_ep)

    def pass_copy(step, d):
        place_xy = (me_xy + n_xy - d) % n_xy
        same_x = x_half == place_xy // (n_xy // 2)
        near, other = jnp.where(same_x, et, across), jnp.where(same_x, across, et)
        rows = rows_in.at[other if step == 2 else near, place_xy]
        return pltpu.make_async_remote_copy(
            rows, rows, fwd_send_sem.at[step, d], fwd_recv_sem.at[step, d],
            device_id=(ep, across if step == 0 else sibling), device_id_type=MESH,
        )

    for d in range(n_xy):
        if d > 0:
            row_copy(d).wait_recv()
        pass_copy(0, d).start()
        pass_copy(1, d).start()

    lane = lax.broadcasted_iota(jnp.int32, (tok, 128), 1).astype(F32)

    @pl.loop(0, NZ)
    def _(z):
        table = idx_recv[z].T
        places, weights = table[:, 0:n_xy], table[:, n_xy : 2 * n_xy]
        at_rest = jnp.where(places >= float(low), places + (z * rest - low).astype(F32), -100000.0)
        at_low = jnp.where(places < float(low), places, -100000.0)
        per_tile = 128 // rest_rows
        total = jnp.zeros((tok, 128), F32)
        for j in range(n_xy):
            total = jnp.where(at_low[:, j : j + 1] + float(j * low) == lane, weights[:, j : j + 1], total)
        combine[z, :, 0:128] = total.astype(BF16)
        for tile in range(n_xy // per_tile):
            total = jnp.zeros((tok, 128), F32)
            for v in range(per_tile):
                j = tile * per_tile + v
                total = jnp.where(
                    at_rest[:, j : j + 1] + float(v * rest_rows) == lane, weights[:, j : j + 1], total
                )
            combine[z, :, (tile + 1) * 128 : (tile + 2) * 128] = total.astype(BF16)

    for d in range(n_xy):
        pass_copy(0, d).wait_recv()
        pass_copy(2, d).start()
    for d in range(n_xy):
        pass_copy(1, d).wait_recv()
        pass_copy(2, d).wait_recv()

    n_part = hid_send_sem.shape[1]
    part_rows = n_rows // n_part
    chunk_lines = n_xy // n_part
    block = hid.shape[2]

    def product(k, q):
        total = jnp.zeros((part_rows, block), F32)
        for v in range(4):
            left = rows_in[v, pl.ds(q * chunk_lines, chunk_lines)].reshape(part_rows, width)
            right = gu_recv[k, pl.ds(v * (n_ep // 4), n_ep // 4)].reshape(width, block)
            total = total + jnp.dot(left, right, preferred_element_type=F32)
        return total

    def hidden_copy(step, q):
        where = pl.ds(q * part_rows, part_rows)
        rows = hid.at[across if step == 2 else et, where]
        return pltpu.make_async_remote_copy(
            rows, rows, hid_send_sem.at[step, q], hid_recv_sem.at[step, q],
            device_id=(ep, across if step == 0 else sibling), device_id_type=MESH,
        )

    wait_weights(0)
    wait_weights(1)

    @pl.loop(0, n_part)
    def _(q):
        where = pl.ds(pl.multiple_of(q * part_rows, part_rows), part_rows)
        g = product(0, q)
        u = product(1, q)
        hid[et, where] = (g / (1.0 + jnp.exp(-g)) * u).astype(BF16)
        hidden_copy(0, q).start()
        hidden_copy(1, q).start()

    @pl.loop(0, n_part)
    def _(q):
        hidden_copy(0, q).wait_recv()
        hidden_copy(2, q).start()

    wait_weights(2)

    def out_copy(i, d, f):
        lanes = pl.ds(features[f][0], features[f][1])
        return pltpu.make_async_remote_copy(
            out_send.at[i, :, lanes], ret.at[me_xy, :, lanes], out_send_sem.at[d, f], ret_recv_sem.at[d, f],
            device_id=(i * NZ + me_z, et), device_id_type=MESH,
        )

    def down_chunk(q):
        hidden_copy(1, q).wait_recv()
        hidden_copy(2, q).wait_recv()
        where = pl.ds(pl.multiple_of(q * part_rows, part_rows), part_rows)
        total = jnp.zeros((part_rows, width), F32)
        for k in range(4):
            right = down_recv[k].reshape(width, block)
            total = total + lax.dot_general(
                hid[k, where], right, (((1,), (1,)), ((), ())), preferred_element_type=F32
            )
        total = total.astype(BF16)
        for v in range(chunk_lines):
            i = q * chunk_lines + v
            rows = total[v * line_rows : (v + 1) * line_rows]
            d = (i - me_xy + n_xy) % n_xy

            @pl.when(d == 0)
            def _():
                ret[me_xy] = rows

            @pl.when(d != 0)
            def _():
                out_send[i] = rows
                out_copy(i, d, 0).start()

    @pl.loop(0, n_part)
    def _(q):
        down_chunk(q)

    for f in range(1, len(features)):
        for d in range(1, n_xy):
            out_copy((me_xy + d) % n_xy, d, f).start()

    def line_sum(z, f):
        lanes = pl.ds(features[f][0], features[f][1])
        where = pl.ds(pl.multiple_of(z * low, low), low)
        near = ret[:, where, lanes].reshape(n_xy * low, features[f][1])
        return rest_sum[z, :, lanes] + jnp.dot(
            combine[z, :, 0:128], near, preferred_element_type=F32
        )

    def rest_sums(f):
        lanes = pl.ds(features[f][0], features[f][1])
        others = ret[:, low_rows:line_rows, lanes].reshape(n_xy * rest_rows, features[f][1])

        @pl.loop(0, 2)
        def _(v):
            zs = pl.ds(v * (NZ // 2), NZ // 2)
            left = combine[zs, :, 128:].reshape(NZ // 2 * tok, n_xy * rest_rows)
            total = jnp.dot(left, others, preferred_element_type=F32)
            rest_sum[zs, :, lanes] = total.reshape(NZ // 2, tok, features[f][1])

    def sum_copy(way, k, f):
        side = 0 if way > 0 else 1
        start, size = (0, tok) if k < far else ((0, half_tok) if way > 0 else (half_tok, half_tok))
        lanes = pl.ds(features[f][0], features[f][1])
        return pltpu.make_async_remote_copy(
            ring_send.at[side, k - 1, pl.ds(start, size), lanes],
            ring_recv.at[side, k - 1, pl.ds(start, size), lanes],
            ring_send_sem.at[side, k - 1, f], ring_recv_sem.at[side, k - 1, f],
            device_id=(me_xy * NZ + (me_z + way) % NZ, et), device_id_type=MESH,
        )

    def ring_step(k, f):
        lanes = pl.ds(features[f][0], features[f][1])
        if k == far:
            if f == 0 or len(features) > 1:
                for d in range(1, n_xy):
                    out_copy((me_xy + d) % n_xy, d, f).wait_recv()
            rest_sums(f)
            total = line_sum((me_z + far) % NZ, f).astype(BF16)
            for side, way in ((0, 1), (1, -1)):
                start = side * half_tok
                ring_send[side, k - 1, start : start + half_tok, lanes] = total[start : start + half_tok]
                sum_copy(way, k, f).start()
            return
        for side, way in ((0, 1), (1, -1)):
            total = line_sum((me_z + way * k) % NZ, f)
            sum_copy(way, k + 1, f).wait_recv()
            if k + 1 == far:
                start = side * half_tok
                other = half_tok - start
                ring_send[side, k - 1, start : start + half_tok, lanes] = (
                    total[start : start + half_tok]
                    + ring_recv[side, k, start : start + half_tok, lanes].astype(F32)
                ).astype(BF16)
                ring_send[side, k - 1, other : other + half_tok, lanes] = total[
                    other : other + half_tok
                ].astype(BF16)
            else:
                ring_send[side, k - 1, :, lanes] = (
                    total + ring_recv[side, k, :, lanes].astype(F32)
                ).astype(BF16)
            sum_copy(way, k, f).start()

    def finish(f):
        lanes = pl.ds(features[f][0], features[f][1])
        total = line_sum(me_z, f)
        for side, way in ((0, 1), (1, -1)):
            sum_copy(way, 1, f).wait_recv()
            total = total + ring_recv[side, 0, :, lanes].astype(F32)
        out_ref[:, lanes] = total.astype(BF16)

    lag = 2
    for t in range(far + lag * (len(features) - 1) + 1):
        for f in range(len(features)):
            s = t - lag * f
            if 0 <= s < far:
                ring_step(far - s, f)
            elif s == far:
                finish(f)

    for d in range(1, NZ):
        index_copy(d).wait_send()
    for way in (1, -1):
        for s in range(1, far + 1):
            token_copy(way, s).wait_send()
            for f in range(len(features)):
                sum_copy(way, s, f).wait_send()
    for d in range(1, n_xy):
        row_copy(d).wait_send()
        for f in range(len(features)):
            out_copy((me_xy + d) % n_xy, d, f).wait_send()
    for d in range(n_xy):
        for step in range(3):
            pass_copy(step, d).wait_send()
    for k in range(3):
        wait_weights_sent(k)

    @pl.loop(0, n_part)
    def _(q):
        for step in range(3):
            hidden_copy(step, q).wait_send()


def per_device(
    tokens, slot_ids, gate_weights, old_expert, new_expert, gate_proj, up_proj, down_proj
):
    n_ep = lax.axis_size("ep")
    n_xy = n_ep // NZ
    tok, width = tokens.shape
    top = slot_ids.shape[1]
    slots, depth, block = gate_proj.shape
    cap = min(tok, (tok * top * 5 + 4 * n_ep - 1) // (4 * n_ep))
    slot_index = jnp.arange(slots, dtype=jnp.int32)
    holders = new_expert[:, None] == old_expert[None, :]
    source = jnp.min(jnp.where(holders, slot_index[None, :], slots - 1), axis=1).astype(jnp.int32)
    line_rows = NZ * cap
    n_rows = n_xy * line_rows
    n_part = 4
    features = ((0, 512), (512, width - 512))
    n_feat = len(features)
    dma = pltpu.SemaphoreType.DMA
    scratch = [
        pltpu.VMEM((slots, depth, block), BF16),
        pltpu.VMEM((slots, depth, block), BF16),
        pltpu.VMEM((slots, depth, block), BF16),
        pltpu.VMEM((3, slots, depth, block), BF16),
        pltpu.VMEM((2, n_ep, depth, block), BF16),
        pltpu.VMEM((4, n_ep // 4, depth, block), BF16),
        pltpu.VMEM((NZ, 2 * n_xy, tok), F32),
        pltpu.VMEM((NZ, 2 * n_xy, tok), F32),
        pltpu.VMEM((NZ, tok, width), BF16),
        pltpu.VMEM((n_xy * NZ * (cap - 16), NZ * tok), BF16),
        pltpu.VMEM((NZ, tok, n_xy * (16 + NZ * (cap - 16))), BF16),
        pltpu.VMEM((n_xy, line_rows, width), BF16),
        pltpu.VMEM((4, n_xy, line_rows, width), BF16),
        pltpu.VMEM((4, n_rows, block), BF16),
        pltpu.VMEM((n_xy, line_rows, width), BF16),
        pltpu.VMEM((n_xy, line_rows, width), BF16),
        pltpu.VMEM((NZ, tok, width), F32),
        pltpu.VMEM((2, NZ // 2, tok, width), BF16),
        pltpu.VMEM((2, NZ // 2, tok, width), BF16),
        dma((4,)), dma((3,)), dma((3,)), dma((2, NZ // 2 + 1)), dma((2, NZ // 2 + 1)), dma((NZ,)), dma((NZ,)),
        dma((n_xy,)), dma((n_xy,)), dma((3, n_xy)), dma((3, n_xy)),
        dma((3, n_part)), dma((3, n_part)), dma((n_xy, n_feat)), dma((n_xy, n_feat)),
        dma((2, NZ // 2, n_feat)), dma((2, NZ // 2, n_feat)),
    ]
    vmem = pl.BlockSpec(memory_space=pltpu.VMEM)
    hbm = pl.BlockSpec(memory_space=pl.ANY)
    return pl.pallas_call(
        functools.partial(layer_kernel, cap, features),
        out_shape=jax.ShapeDtypeStruct((tok, width), BF16),
        in_specs=[pl.BlockSpec(memory_space=pltpu.SMEM), hbm, vmem, vmem, hbm, hbm, hbm],
        out_specs=vmem,
        scratch_shapes=scratch,
        compiler_params=pltpu.CompilerParams(
            collective_id=0, has_side_effects=True, vmem_limit_bytes=60 * 1024 * 1024
        ),
        name="moe_layer",
    )(source, tokens, slot_ids.T, gate_weights.T, gate_proj, up_proj, down_proj)


def solution(mesh):
    placed = (
        P("ep", "et"), P("ep", None), P("ep", None), P(), P(),
        P(None, "ep", "et"), P(None, "ep", "et"), P(None, "ep", "et"),
    )
    return jax.shard_map(
        per_device, mesh=mesh, in_specs=placed, out_specs=P("ep", "et"), check_vma=False
    )
```
